32 devices in a mesh: blk: 8 (over y, x, core), grp: 4 (over z).
Axes of the slice: x: 2, y: 2, z: 4, core: 2. Of those that a mesh axis runs over, the one named last changes fastest.
Arguments:
- picture_embedding: bfloat16 [12288, 1152], P(('blk', 'grp')), may hold values from -1.5 to 1.5
- caption_embedding: bfloat16 [12288, 1152], P(('blk', 'grp')), may hold values from -1.5 to 1.5
- inverse_warmth: float32 [], replicated, may hold values from 2 to 10
- additive_offset: float32 [], replicated, may hold values from -4 to 0
- matching_caption_group: int32 [12288], P(('blk', 'grp')), may hold values from 0 to 2
- matching_caption_entry: int32 [12288], P(('blk', 'grp')), may hold values from 0 to 383
Outputs:
- grad_image: bfloat16 [12288, 1152], P(('blk', 'grp'))
- grad_text: bfloat16 [12288, 1152], P(('blk', 'grp'))
The draws below stay inside these ranges and needn't reach their ends.
Inputs may be any that keep to these rules, and one draw needn't show every extreme that they name: matching_caption_group[i] names the window block k - 1 + matching_caption_group[i] of image i's block k.
All inputs are finite; a program needn't handle non-finite values.
Results may differ from the reference program's by a relative error of at most 0.007.
Values may be sent and summed in bfloat16 or wider, within the bound.
A program may use at most 64 MiB of HBM per device.

```python
import math
import jax
import jax.numpy as jnp
from jax import lax

D = 1152
ROWS = 384
BATCH = 12288


def place_ends(entries, stream_key, smallest, top_value):
    shape = entries.shape
    index_at = [jax.random.randint(jax.random.fold_in(stream_key, axis), (), 0, shape[axis]) for axis in range(len(shape))]
    entries = entries.at[tuple(index_at)].set(smallest)
    longest = shape.index(max(shape))
    index_at[longest] = (index_at[longest] + 1) % shape[longest]
    return entries.at[tuple(index_at)].set(top_value)


def shard_levels(own_key, dims, pieces, low, largest):
    def one(dim, blocks):
        steps = jax.random.uniform(jax.random.fold_in(jax.random.fold_in(own_key, 6), dim), (blocks,), jnp.float32, low / len(pieces), largest / len(pieces))
        return jnp.repeat(jnp.exp(steps), dims[dim] // blocks).reshape((-1,) + (1,) * (len(dims) - dim - 1))

    level = one(*pieces[0])
    for cut in pieces[1:]:
        level = level * one(*cut)
    return level


def gaussian(own_key, extent, spread, limit, split=(), kind=jnp.bfloat16):
    result = jax.random.normal(own_key, extent, jnp.float32) * spread
    if len(split) > 0:
        result = shard_levels(own_key, extent, split, -0.22, 0.18) * result
    return jnp.clip(result, min=-limit, max=limit).astype(kind)


def setup_inputs(seed: int = 0) -> dict:
    arg_keys = jax.random.split(jax.random.key(seed), 7)
    return {
        "picture_embedding": gaussian(arg_keys[0], (BATCH, D), (0.55 * D ** -0.25), 1.5, ((0, 32),)),
        "caption_embedding": gaussian(arg_keys[1], (BATCH, D), (0.55 * D ** -0.25), 1.5, ((0, 32),)),
        "inverse_warmth": jnp.clip(jnp.exp(jax.random.uniform(arg_keys[2], (), jnp.float32, math.log(2.0), math.log(10.0))), 2.0, 10.0),
        "additive_offset": jnp.clip(jax.random.uniform(arg_keys[3], (), jnp.float32, -4.0, 0.0), -4.0, 0.0),
        "matching_caption_group": place_ends(jax.random.randint(arg_keys[4], (BATCH,), 0, 3), jax.random.fold_in(arg_keys[4], 1), 0, 2).astype(jnp.int32),
        "matching_caption_entry": place_ends(jax.random.randint(arg_keys[5], (BATCH,), 0, ROWS), jax.random.fold_in(arg_keys[5], 1), 0, ROWS - 1).astype(jnp.int32),
    }


def logistic_slices(picture_entries, adjacent_reach, target_signs, inverse_warmth, additive_offset):
    similarity_values = jnp.dot(picture_entries, adjacent_reach.T, preferred_element_type=jnp.float32)
    similarity_raw = inverse_warmth * similarity_values + additive_offset
    column_index = lax.broadcasted_iota(jnp.int32, similarity_raw.shape, 1)
    pair_sign = jnp.where(column_index == target_signs[:, None], jnp.float32(1.0), jnp.float32(-1.0))
    return (-pair_sign * jax.nn.sigmoid(-pair_sign * similarity_raw)).astype(jnp.bfloat16)


def reference(picture_embedding, caption_embedding, inverse_warmth, additive_offset, matching_caption_group, matching_caption_entry):
    block_count = BATCH // ROWS
    image_blocks = picture_embedding.reshape(block_count, ROWS, D)
    text_blocks = caption_embedding.reshape(block_count, ROWS, D)
    targets = (matching_caption_group * ROWS + matching_caption_entry).astype(jnp.int32).reshape(block_count, ROWS)

    def step(accumulated, block_index):
        before = (block_index - 1 + block_count) % block_count
        after = (block_index + 1) % block_count
        adjacent_reach = jnp.concatenate([
            lax.dynamic_index_in_dim(text_blocks, before, 0, keepdims=False),
            lax.dynamic_index_in_dim(text_blocks, block_index, 0, keepdims=False),
            lax.dynamic_index_in_dim(text_blocks, after, 0, keepdims=False)], axis=0)
        picture_entries = lax.dynamic_index_in_dim(image_blocks, block_index, 0, keepdims=False)
        target_signs = lax.dynamic_index_in_dim(targets, block_index, 0, keepdims=False)
        derivative_slices = logistic_slices(picture_entries, adjacent_reach, target_signs, inverse_warmth, additive_offset)
        picture_derivative = (inverse_warmth * jnp.dot(derivative_slices, adjacent_reach, preferred_element_type=jnp.float32)).astype(jnp.bfloat16)
        incomplete_portion = inverse_warmth * jnp.dot(derivative_slices.T, picture_entries, preferred_element_type=jnp.float32)
        accumulated = accumulated.at[before].add(incomplete_portion[:ROWS])
        accumulated = accumulated.at[block_index].add(incomplete_portion[ROWS:2 * ROWS])
        accumulated = accumulated.at[after].add(incomplete_portion[2 * ROWS:])
        return accumulated, picture_derivative

    start = jnp.zeros((block_count, ROWS, D), jnp.float32)
    accumulated, image_grads = lax.scan(step, start, jnp.arange(block_count, dtype=jnp.int32))
    grad_image = image_grads.reshape(BATCH, D)
    grad_text = accumulated.reshape(BATCH, D).astype(jnp.bfloat16)
    return grad_image, grad_text
```

```python
import functools

import jax
import jax.numpy as jnp
from jax import lax
from jax.experimental import pallas as pl
from jax.experimental.pallas import tpu as pltpu
from jax.sharding import PartitionSpec as P

MESH = pl.DeviceIdType.MESH
LANES = 128
WINDOW = 2


def kernel(
    axes,
    sizes,
    pieces,
    group_ref,
    entry_ref,
    warmth_ref,
    offset_ref,
    picture_hbm,
    caption_hbm,
    grad_image_ref,
    grad_text_ref,
    picture,
    caption,
    target,
    far_picture,
    far_caption,
    far_target,
    image_sum,
    text_sum,
    local_sem,
    send_sem,
    recv_sem,
):
    rows = picture.shape[0]
    outer, inner = sizes
    count = outer * inner
    me = lax.axis_index(axes[0]) * inner + lax.axis_index(axes[1])

    def place(index):
        return {axes[0]: index // inner, axes[1]: lax.rem(index, inner)}

    right = place(lax.rem(me + 1, count))
    left = place(lax.rem(me + count - 1, count))

    barrier = pltpu.get_barrier_semaphore()
    for neighbour in (left, right):
        pl.semaphore_signal(barrier, inc=1, device_id=neighbour, device_id_type=MESH)
    load_picture = pltpu.make_async_copy(picture_hbm, picture, local_sem.at[0])
    load_caption = pltpu.make_async_copy(caption_hbm, caption, local_sem.at[1])
    load_picture.start()
    load_caption.start()
    target[...] = jnp.broadcast_to(
        group_ref[...] * rows + entry_ref[...], target.shape
    )
    pl.semaphore_wait(barrier, 2)

    def send(piece, slot):
        kind, start, size = pieces[piece]
        if kind == "target":
            source, sink = target, far_target.at[slot]
        elif kind == "caption":
            source = caption_hbm.at[pl.ds(start, size)]
            sink = far_caption.at[slot, pl.ds(start, size)]
        else:
            source = picture_hbm.at[pl.ds(start, size)]
            sink = far_picture.at[slot, pl.ds(start, size)]
        return pltpu.make_async_remote_copy(
            src_ref=source,
            dst_ref=sink,
            send_sem=send_sem.at[slot, piece],
            recv_sem=recv_sem.at[slot, piece],
            device_id=(right, left)[slot],
            device_id_type=MESH,
        )

    sends = [[send(piece, slot) for slot in (0, 1)] for piece in range(len(pieces))]
    started = 0
    for piece in range(min(1 + WINDOW, len(pieces))):
        for copy in sends[piece]:
            copy.start()
        started += 1
    sent = 0

    warmth = warmth_ref[0]
    offset = offset_ref[0]

    def tile(text, image, image_target, first):
        logit = warmth * lax.dot_general(
            text, image, (((1,), (1,)), ((), ())), preferred_element_type=jnp.float32
        ) + offset
        row = lax.broadcasted_iota(jnp.int32, logit.shape, 0) + first
        match = row == image_target
        value = jax.nn.sigmoid(jnp.where(match, -logit, logit))
        return jnp.where(match, -value, value).astype(jnp.bfloat16)

    def over_text(values, text):
        return lax.dot_general(
            values, text, (((0,), (0,)), ((), ())), preferred_element_type=jnp.float32
        )

    load_picture.wait()
    load_caption.wait()
    own = tile(caption[...], picture[...], target[0:1, :], rows)
    text_sum[...] = jnp.dot(own, picture[...], preferred_element_type=jnp.float32)
    image_sum[...] = over_text(own, caption[...])

    captions_left = sum(kind == "caption" for kind, _, _ in pieces)
    for piece, (kind, start, size) in enumerate(pieces):
        if piece >= 1 and started < len(pieces):
            for copy in sends[piece]:
                copy.wait_send()
            sent = piece + 1
            for copy in sends[started]:
                copy.start()
            started += 1
        for slot in (0, 1):
            sends[piece][slot].wait_recv()
            if kind == "caption":
                text = far_caption[slot, pl.ds(start, size)]
                values = tile(text, picture[...], target[0:1, :], 2 * slot * rows + start)
                image_sum[...] += over_text(values, text)
            elif kind == "picture":
                image = far_picture[slot, pl.ds(start, size)]
                values = tile(
                    caption[...],
                    image,
                    far_target[slot, 0:1, pl.ds(start, size)],
                    2 * (1 - slot) * rows,
                )
                text_sum[...] += jnp.dot(
                    values, image, preferred_element_type=jnp.float32
                )
        if kind == "caption":
            captions_left -= 1
            if captions_left == 0:
                grad_image_ref[...] = (warmth * image_sum[...]).astype(
                    grad_image_ref.dtype
                )
    grad_text_ref[...] = (warmth * text_sum[...]).astype(grad_text_ref.dtype)
    for piece in range(len(pieces)):
        if piece == 0 or piece >= sent:
            for copy in sends[piece]:
                copy.wait_send()


def per_device(
    axes,
    sizes,
    picture_embedding,
    caption_embedding,
    inverse_warmth,
    additive_offset,
    matching_caption_group,
    matching_caption_entry,
):
    rows, width = picture_embedding.shape
    chunk = LANES if rows % LANES == 0 else rows
    pieces = [("target", 0, rows), ("caption", 0, rows)]
    pieces += [("picture", start, chunk) for start in range(0, rows, chunk)]
    block = (rows, width)
    vmem = pl.BlockSpec(memory_space=pltpu.VMEM)
    smem = pl.BlockSpec(memory_space=pltpu.SMEM)
    hbm = pl.BlockSpec(memory_space=pl.ANY)
    out = jax.ShapeDtypeStruct(block, jnp.bfloat16)
    return pl.pallas_call(
        functools.partial(kernel, axes, sizes, pieces),
        out_shape=(out, out),
        in_specs=[vmem, vmem, smem, smem, hbm, hbm],
        out_specs=(vmem, vmem),
        scratch_shapes=[
            pltpu.VMEM(block, jnp.bfloat16),
            pltpu.VMEM(block, jnp.bfloat16),
            pltpu.VMEM((8, rows), jnp.int32),
            pltpu.VMEM((2,) + block, jnp.bfloat16),
            pltpu.VMEM((2,) + block, jnp.bfloat16),
            pltpu.VMEM((2, 8, rows), jnp.int32),
            pltpu.VMEM(block, jnp.float32),
            pltpu.VMEM(block, jnp.float32),
            pltpu.SemaphoreType.DMA((2,)),
            pltpu.SemaphoreType.DMA((2, len(pieces))),
            pltpu.SemaphoreType.DMA((2, len(pieces))),
        ],
        compiler_params=pltpu.CompilerParams(
            collective_id=0, has_side_effects=True, vmem_limit_bytes=32 << 20
        ),
    )(
        matching_caption_group.reshape(1, rows),
        matching_caption_entry.reshape(1, rows),
        inverse_warmth.reshape(1),
        additive_offset.reshape(1),
        picture_embedding,
        caption_embedding,
    )


def solution(mesh):
    axes = ("blk", "grp")
    sizes = tuple(mesh.shape[axis] for axis in axes)
    placed = (
        P(axes, None),
        P(axes, None),
        P(),
        P(),
        P(axes),
        P(axes),
    )
    return jax.shard_map(
        functools.partial(per_device, axes, sizes),
        mesh=mesh,
        in_specs=placed,
        out_specs=(P(axes, None), P(axes, None)),
        check_vma=False,
    )
```

```python
import functools

import jax
import jax.numpy as jnp
from jax import lax
from jax.experimental import pallas as pl
from jax.experimental.pallas import tpu as pltpu
from jax.sharding import PartitionSpec as P

MESH = pl.DeviceIdType.MESH
LANES = 128
WINDOW = 2


def kernel(
    axes,
    sizes,
    pieces,
    group_hbm,
    entry_hbm,
    warmth_ref,
    offset_ref,
    picture_hbm,
    caption_hbm,
    grad_image_ref,
    grad_text_ref,
    group_ref,
    entry_ref,
    picture,
    caption,
    target,
    far_picture,
    far_caption,
    far_target,
    image_sum,
    text_sum,
    local_sem,
    send_sem,
    recv_sem,
):
    rows = picture.shape[0]
    outer, inner = sizes
    count = outer * inner
    me = lax.axis_index(axes[0]) * inner + lax.axis_index(axes[1])

    def place(index):
        return {axes[0]: index // inner, axes[1]: lax.rem(index, inner)}

    right = place(lax.rem(me + 1, count))
    left = place(lax.rem(me + count - 1, count))

    barrier = pltpu.get_barrier_semaphore()
    for neighbour in (left, right):
        pl.semaphore_signal(barrier, inc=1, device_id=neighbour, device_id_type=MESH)
    loads = [
        pltpu.make_async_copy(source, sink, local_sem.at[index])
        for index, (source, sink) in enumerate(
            (
                (group_hbm, group_ref),
                (entry_hbm, entry_ref),
                (picture_hbm, picture),
                (caption_hbm, caption),
            )
        )
    ]
    for load in loads:
        load.start()
    loads[0].wait()
    loads[1].wait()
    target[...] = jnp.broadcast_to(
        (group_ref[...] * rows + entry_ref[...]).reshape(1, rows), target.shape
    )
    pl.semaphore_wait(barrier, 2)

    def send(piece, slot):
        kind, start, size = pieces[piece]
        if kind == "target":
            source, sink = target, far_target.at[slot]
        elif kind == "caption":
            source = caption_hbm.at[pl.ds(start, size)]
            sink = far_caption.at[slot, pl.ds(start, size)]
        else:
            source = picture_hbm.at[pl.ds(start, size)]
            sink = far_picture.at[slot, pl.ds(start, size)]
        return pltpu.make_async_remote_copy(
            src_ref=source,
            dst_ref=sink,
            send_sem=send_sem.at[slot, piece],
            recv_sem=recv_sem.at[slot, piece],
            device_id=(right, left)[slot],
            device_id_type=MESH,
        )

    sends = [[send(piece, slot) for slot in (0, 1)] for piece in range(len(pieces))]
    started = 0
    for piece in range(min(1 + WINDOW, len(pieces))):
        for copy in sends[piece]:
            copy.start()
        started += 1
    sent = 0

    for load in loads[2:]:
        load.wait()
    warmth = warmth_ref[0]
    offset = offset_ref[0]

    def tile(text, image, image_target, first):
        logit = warmth * lax.dot_general(
            text, image, (((1,), (1,)), ((), ())), preferred_element_type=jnp.float32
        ) + offset
        row = lax.broadcasted_iota(jnp.int32, logit.shape, 0) + first
        match = row == image_target
        value = jax.nn.sigmoid(jnp.where(match, -logit, logit))
        return jnp.where(match, -value, value).astype(jnp.bfloat16)

    def over_text(values, text):
        return lax.dot_general(
            values, text, (((0,), (0,)), ((), ())), preferred_element_type=jnp.float32
        )

    own = tile(caption[...], picture[...], target[0:1, :], rows)
    text_sum[...] = jnp.dot(own, picture[...], preferred_element_type=jnp.float32)
    image_sum[...] = over_text(own, caption[...])

    captions_left = sum(kind == "caption" for kind, _, _ in pieces)
    for piece, (kind, start, size) in enumerate(pieces):
        if piece >= 1 and started < len(pieces):
            for copy in sends[piece]:
                copy.wait_send()
            sent = piece + 1
            for copy in sends[started]:
                copy.start()
            started += 1
        for slot in (0, 1):
            sends[piece][slot].wait_recv()
            if kind == "caption":
                text = far_caption[slot, pl.ds(start, size)]
                values = tile(text, picture[...], target[0:1, :], 2 * slot * rows + start)
                image_sum[...] += over_text(values, text)
            elif kind == "picture":
                image = far_picture[slot, pl.ds(start, size)]
                values = tile(
                    caption[...],
                    image,
                    far_target[slot, 0:1, pl.ds(start, size)],
                    2 * (1 - slot) * rows,
                )
                text_sum[...] += jnp.dot(
                    values, image, preferred_element_type=jnp.float32
                )
        if kind == "caption":
            captions_left -= 1
            if captions_left == 0:
                grad_image_ref[...] = (warmth * image_sum[...]).astype(
                    grad_image_ref.dtype
                )
    grad_text_ref[...] = (warmth * text_sum[...]).astype(grad_text_ref.dtype)
    for piece in range(len(pieces)):
        if piece == 0 or piece >= sent:
            for copy in sends[piece]:
                copy.wait_send()


def store(image_ref, text_ref, image_hbm, text_hbm, sem):
    copies = [
        pltpu.make_async_copy(image_ref, image_hbm, sem.at[0]),
        pltpu.make_async_copy(text_ref, text_hbm, sem.at[1]),
    ]
    for copy in copies:
        copy.start()
    for copy in copies:
        copy.wait()


def per_device(
    axes,
    sizes,
    picture_embedding,
    caption_embedding,
    inverse_warmth,
    additive_offset,
    matching_caption_group,
    matching_caption_entry,
):
    rows, width = picture_embedding.shape
    chunk = LANES if rows % LANES == 0 else rows
    pieces = [("target", 0, rows), ("caption", 0, rows)]
    pieces += [("picture", start, chunk) for start in range(0, rows, chunk)]
    block = (rows, width)
    vmem = pl.BlockSpec(memory_space=pltpu.VMEM)
    smem = pl.BlockSpec(memory_space=pltpu.SMEM)
    hbm = pl.BlockSpec(memory_space=pltpu.HBM)
    grad_image, grad_text = pl.pallas_call(
        functools.partial(kernel, axes, sizes, pieces),
        out_shape=(pltpu.VMEM(block, jnp.bfloat16), pltpu.VMEM(block, jnp.bfloat16)),
        in_specs=[hbm, hbm, smem, smem, hbm, hbm],
        out_specs=(vmem, vmem),
        scratch_shapes=[
            pltpu.VMEM((rows,), jnp.int32),
            pltpu.VMEM((rows,), jnp.int32),
            pltpu.VMEM(block, jnp.bfloat16),
            pltpu.VMEM(block, jnp.bfloat16),
            pltpu.VMEM((8, rows), jnp.int32),
            pltpu.VMEM((2,) + block, jnp.bfloat16),
            pltpu.VMEM((2,) + block, jnp.bfloat16),
            pltpu.VMEM((2, 8, rows), jnp.int32),
            pltpu.VMEM(block, jnp.float32),
            pltpu.VMEM(block, jnp.float32),
            pltpu.SemaphoreType.DMA((4,)),
            pltpu.SemaphoreType.DMA((2, len(pieces))),
            pltpu.SemaphoreType.DMA((2, len(pieces))),
        ],
        compiler_params=pltpu.CompilerParams(
            collective_id=0, has_side_effects=True, vmem_limit_bytes=32 << 20
        ),
    )(
        pltpu.with_memory_space_constraint(matching_caption_group, pltpu.HBM),
        pltpu.with_memory_space_constraint(matching_caption_entry, pltpu.HBM),
        inverse_warmth.reshape(1),
        additive_offset.reshape(1),
        pltpu.with_memory_space_constraint(picture_embedding, pltpu.HBM),
        pltpu.with_memory_space_constraint(caption_embedding, pltpu.HBM),
    )
    return pl.pallas_call(
        store,
        out_shape=(pltpu.HBM(block, jnp.bfloat16), pltpu.HBM(block, jnp.bfloat16)),
        in_specs=[vmem, vmem],
        out_specs=(hbm, hbm),
        scratch_shapes=[pltpu.SemaphoreType.DMA((2,))],
    )(
        pltpu.with_memory_space_constraint(grad_image, pltpu.VMEM),
        pltpu.with_memory_space_constraint(grad_text, pltpu.VMEM),
    )


def solution(mesh):
    axes = ("blk", "grp")
    sizes = tuple(mesh.shape[axis] for axis in axes)
    placed = (
        P(axes, None),
        P(axes, None),
        P(),
        P(),
        P(axes),
        P(axes),
    )
    return jax.shard_map(
        functools.partial(per_device, axes, sizes),
        mesh=mesh,
        in_specs=placed,
        out_specs=(P(axes, None), P(axes, None)),
        check_vma=False,
    )
```
